32 devices in a mesh: members: 2 (over x), nodes: 16 (over z, y, core).
Axes of the slice: x: 2, y: 2, z: 4, core: 2. Of those that a mesh axis runs over, the one named last changes fastest.
Arguments:
- wave_state: float32 [16384, 1296], P(('members', 'nodes')), parts along dimension 0, may hold values from -6 to 6
- pool_weight: float32 [8192], P('nodes'), may hold values from -0.5 to 0.5
- lift_weight: float32 [8192], P('nodes'), may hold values from -8 to 8
- coarse_matrix: bfloat16 [64, 64], replicated, may hold values from -0.75 to 0.75
- block_matrix: float32 [16, 20, 128, 128], P('nodes'), may hold values from -0.25 to 0.25
- edge_dst: int32 [16, 20], P('nodes'), may hold values from 0 to 3
- edge_src: int32 [16, 20], P('nodes'), may hold values from 0 to 11
- edge_count: int32 [16], P('nodes'), may hold values from 10 to 20, as said below
- send_list: int32 [16, 4, 2], P('nodes'), may hold values from 0 to 3
- norm_gain: float32 [1296], replicated, may hold values from 0.1 to 1.9
- proj_in: bfloat16 [1296, 1024], replicated, may hold values from -0.15625 to 0.15625
- proj_out: bfloat16 [1024, 1296], replicated, may hold values from -0.1875 to 0.1875
Outputs:
- next_state: float32 [16384, 1296], P(('members', 'nodes')), parts along dimension 0
The draws below stay inside these ranges and needn't reach their ends.
There are 2 independent parts, one for each index of `members`. The reference program is written for one: setup_inputs(seed, part) draws one part's arguments, and reference() takes and returns one part's arrays. A program takes and returns all parts, laid end to end along the dimension named above; an argument that names none is the same for every part. Nothing has to cross between parts.
Inputs may be any that keep to these rules, and one draw needn't show every extreme that they name: `edge_count`: some partition has all 20 slots live.
All inputs are finite; a program needn't handle non-finite values.
Results may differ from the reference program's by a relative error of at most 0.0028.
Values may be sent and summed in bfloat16 or wider, within the bound.
A program may use at most 128 MiB of HBM per device.

```python
import jax
import jax.numpy as jnp
from jax import lax

BINS = 1296
HIDDEN_SIZE = 1024
BLOCK = 128
SENDS = 2
EDGES_BLOCK = 5
BLOCKS_DEV = 4
PARTITIONS = 16
EDGES = 20
ALL_BLOCKS = 64
NODES = 8192


def draw_edge_count(key, part):
    key = jax.random.fold_in(key, 7)
    first_key, second_key = jax.random.split(key)
    counts = jax.random.randint(first_key, (PARTITIONS,), EDGES // 2, EDGES + 1)
    full_part = jax.random.randint(second_key, (), 0, PARTITIONS)
    return jnp.where(jnp.arange(PARTITIONS) == full_part, EDGES, counts).astype(jnp.int32)


def plant(values, key, least, top_value):
    extent = values.shape
    index_at = [jax.random.randint(jax.random.fold_in(key, axis), (), 0, extent[axis]) for axis in range(len(extent))]
    values = values.at[tuple(index_at)].set(least)
    longest = extent.index(max(extent))
    index_at[longest] = (index_at[longest] + 1) % extent[longest]
    return values.at[tuple(index_at)].set(top_value)


def level_of(stream_key, extent, cuts, low, largest):
    def one(dim, blocks):
        steps = jax.random.uniform(jax.random.fold_in(jax.random.fold_in(stream_key, 6), dim), (blocks,), jnp.float32, low / len(cuts), largest / len(cuts))
        return jnp.repeat(jnp.exp(steps), extent[dim] // blocks).reshape((-1,) + (1,) * (len(extent) - dim - 1))

    gain = one(*cuts[0])
    for cut in cuts[1:]:
        gain = gain * one(*cut)
    return gain


def normal_values(stream_key, extent, width, reach, cuts=(), kind=jnp.bfloat16):
    factor_of = level_of(stream_key, extent, cuts, -0.22, 0.18) if cuts else 1.0
    values = jax.random.normal(stream_key, extent, jnp.float32) * width * factor_of
    return jnp.minimum(jnp.maximum(values, -reach), reach).astype(kind)


def setup_inputs(seed: int = 0, part: int = 0) -> dict:
    seeds = jax.random.split(jax.random.key(seed), 13)
    part_splits = jax.random.split(jax.random.fold_in(seeds[12], part), 13)
    return {
        "wave_state": normal_values(part_splits[0], (NODES, BINS), 1.0, 6.0, ((0, 16),), jnp.float32),
        "pool_weight": normal_values(seeds[1], (NODES,), BLOCK ** -0.5, 0.5, ((0, 16),), jnp.float32),
        "lift_weight": normal_values(seeds[2], (NODES,), 2.0, 8.0, ((0, 16),), jnp.float32),
        "coarse_matrix": normal_values(seeds[3], (ALL_BLOCKS, ALL_BLOCKS), ALL_BLOCKS ** -0.5, 0.75),
        "block_matrix": normal_values(seeds[4], (PARTITIONS, EDGES, BLOCK, BLOCK), (BLOCK * EDGES_BLOCK) ** -0.5, 0.25, ((0, 16),), jnp.float32),
        "edge_dst": plant(jax.random.randint(seeds[5], (PARTITIONS, EDGES), 0, BLOCKS_DEV), jax.random.fold_in(seeds[5], 1), 0, BLOCKS_DEV - 1).astype(jnp.int32),
        "edge_src": plant(jax.random.randint(seeds[6], (PARTITIONS, EDGES), 0, BLOCKS_DEV + 4 * SENDS), jax.random.fold_in(seeds[6], 1), 0, (BLOCKS_DEV + 4 * SENDS) - 1).astype(jnp.int32),
        "edge_count": draw_edge_count(jax.random.fold_in(seeds[12], 71), part),
        "send_list": plant(jax.random.randint(seeds[8], (PARTITIONS, 4, SENDS), 0, BLOCKS_DEV), jax.random.fold_in(seeds[8], 1), 0, BLOCKS_DEV - 1).astype(jnp.int32),
        "norm_gain": jnp.clip(1.0 + 0.18 * jax.random.normal(seeds[9], (BINS,), jnp.float32), 0.1, 1.9),
        "proj_in": normal_values(seeds[10], (BINS, HIDDEN_SIZE), BINS ** -0.5, 0.15625),
        "proj_out": normal_values(seeds[11], (HIDDEN_SIZE, BINS), HIDDEN_SIZE ** -0.5, 0.1875),
    }


def reference(wave_state, pool_weight, lift_weight, coarse_matrix, block_matrix, edge_dst, edge_src, edge_count, send_list, norm_gain, proj_in, proj_out):
    grid_all = wave_state.reshape(PARTITIONS, BLOCKS_DEV, BLOCK, BINS)
    pool_view = pool_weight.reshape(PARTITIONS, BLOCKS_DEV, BLOCK)
    lift_view = lift_weight.reshape(PARTITIONS, BLOCKS_DEV, BLOCK)
    pooled = jnp.einsum('pnib,pni->pnb', grid_all, pool_view, precision=lax.Precision.HIGHEST)
    pooled = pooled.astype(jnp.bfloat16).reshape(ALL_BLOCKS, BINS)
    coarse = jnp.dot(coarse_matrix, pooled, preferred_element_type=jnp.float32)
    coarse = coarse.reshape(PARTITIONS, BLOCKS_DEV, BINS)

    def one_part(partition):
        own_blocks = grid_all[partition]
        arrived = []
        for column, offset in enumerate((1, -1, 2, -2)):
            source_part = ((partition - offset) % PARTITIONS).astype(jnp.int32)
            arrived.append(jnp.take(grid_all[source_part], send_list[source_part, column], axis=0))
        extended = jnp.concatenate([own_blocks] + arrived, 0)
        sources = jnp.take(extended, edge_src[partition], axis=0)
        product = jnp.einsum('eij,ejb->eib', block_matrix[partition], sources, precision=lax.Precision.HIGHEST)
        live_mask = (jnp.arange(EDGES, dtype=jnp.int32) < edge_count[partition]).astype(jnp.float32)
        selector = (edge_dst[partition][None, :] == jnp.arange(BLOCKS_DEV, dtype=jnp.int32)[:, None]).astype(jnp.float32)
        selector = selector * live_mask[None, :]
        moved = jnp.einsum('ne,eib->nib', selector, product, precision=lax.Precision.HIGHEST)
        field = own_blocks + moved + lift_view[partition][:, :, None] * coarse[partition][:, None, :]
        flat = field.reshape(BLOCKS_DEV * BLOCK, BINS)
        mean_square = lax.optimization_barrier(jnp.mean(flat * flat, axis=1, keepdims=True))
        normed = (flat * lax.rsqrt(mean_square + 1e-06) * norm_gain).astype(jnp.bfloat16)
        pre_act = jnp.dot(normed, proj_in, preferred_element_type=jnp.float32)
        hidden = jax.nn.gelu(pre_act).astype(jnp.bfloat16)
        return flat + jnp.dot(hidden, proj_out, preferred_element_type=jnp.float32)
    result = lax.map(one_part, jnp.arange(PARTITIONS, dtype=jnp.int32))
    return result.reshape(NODES, BINS)
```

```python
import jax
import jax.numpy as jnp
from jax import lax
from jax.sharding import PartitionSpec as P

BLOCK = 128


def from_behind(shard, axis, by):
    size = lax.axis_size(axis)
    return lax.ppermute(shard, axis, [(i, (i + by) % size) for i in range(size)])


def shards(
    wave_state,
    pool_weight,
    lift_weight,
    coarse_matrix,
    block_matrix,
    edge_dst,
    edge_src,
    edge_count,
    send_list,
    norm_gain,
    proj_in,
    proj_out,
):
    bin_count = wave_state.shape[1]
    blocks_own = wave_state.reshape(-1, BLOCK, bin_count)
    owned_count = blocks_own.shape[0]
    pooled = jnp.einsum(
        "nib,ni->nb",
        blocks_own,
        pool_weight.reshape(owned_count, BLOCK),
        precision=lax.Precision.HIGHEST,
    )
    pooled = pooled.astype(jnp.bfloat16)
    position = lax.axis_index("nodes")
    my_rows = lax.dynamic_slice_in_dim(coarse_matrix, position * owned_count, owned_count, 0)
    coarse = jnp.dot(
        my_rows,
        lax.all_gather(pooled, "nodes", axis=0, tiled=True),
        preferred_element_type=jnp.float32,
    )
    chosen = send_list[0]
    narrow = blocks_own.astype(jnp.bfloat16)
    arrived = [None, None, None, None]
    for column, offset in enumerate((1, -1, 2, -2)):
        arrived[column] = from_behind(jnp.take(narrow, chosen[column], axis=0), "nodes", offset)
    extended = jnp.concatenate([narrow] + arrived, 0)
    sources = jnp.take(extended, edge_src[0], axis=0)
    slot_count = edge_src.shape[1]
    live_mask = jnp.arange(slot_count, dtype=jnp.int32) < edge_count[0]
    selector = (edge_dst[0][None, :] == jnp.arange(owned_count, dtype=jnp.int32)[:, None]) & live_mask[None, :]
    weights = block_matrix[0].transpose(1, 0, 2).reshape(BLOCK, -1).astype(jnp.bfloat16)
    spread = jnp.repeat(selector, BLOCK, axis=1)
    weights = jnp.where(spread[:, None, :], weights[None], 0).reshape(owned_count * BLOCK, -1)
    moved = jnp.dot(weights, sources.reshape(-1, bin_count), preferred_element_type=jnp.float32)
    moved = moved.reshape(owned_count, BLOCK, bin_count)
    field = (
        blocks_own
        + moved
        + lift_weight.reshape(owned_count, BLOCK)[:, :, None] * coarse[:, None, :]
    )
    flat = field.reshape(-1, bin_count)
    mean_square = jnp.mean(flat * flat, axis=1, keepdims=True)
    normed = (flat * lax.rsqrt(mean_square + 1e-06) * norm_gain).astype(jnp.bfloat16)
    pre_act = jnp.dot(normed, proj_in, preferred_element_type=jnp.float32)
    hidden = jax.nn.gelu(pre_act).astype(jnp.bfloat16)
    return flat + jnp.dot(hidden, proj_out, preferred_element_type=jnp.float32)


def solution(mesh):
    in_specs = (
        P(("members", "nodes"), None),
        P("nodes"),
        P("nodes"),
        P(),
        P("nodes", None, None, None),
        P("nodes", None),
        P("nodes", None),
        P("nodes"),
        P("nodes", None, None),
        P(),
        P(),
        P(),
    )
    out_specs = P(("members", "nodes"), None)
    return jax.shard_map(shards, mesh=mesh, in_specs=in_specs, out_specs=out_specs, check_vma=False)
```

```python
import functools

import jax
import jax.numpy as jnp
from jax import lax
from jax.experimental import pallas as pl
from jax.experimental.pallas import tpu as pltpu
from jax.sharding import PartitionSpec as P

BLOCK = 128
PIECE = 384
MESH = pl.DeviceIdType.MESH


def pieces_of(bins):
    out, start = [], 0
    while start < bins:
        width = min(PIECE, bins - start)
        out.append((start, width, -(-width // 128) * 128))
        start += width
    return out


def exchange_kernel(
    size, owned, pieces,
    state, columns, mixing, matrix, edge_dst, edge_src, edge_count, list_ref,
    field,
    weights, gathered, pooled, lists, lists_scalar, coarse,
    own_send, own_recv, list_send, list_recv, pool_send, pool_recv, local_sem,
    *ext,
):
    slots = matrix.shape[0]
    count = len(pieces)
    me = lax.axis_index("nodes")
    core = lax.rem(me, 2)
    chip = me // 2
    odd = lax.rem(chip, 2)
    mate = chip * 2 + 1 - core
    partner = (chip + 1 - 2 * odd) * 2 + core
    onward = lax.rem(me + 4 - 8 * odd + size, size)

    barrier = pltpu.get_barrier_semaphore()

    def greet(step, carry):
        pl.semaphore_signal(
            barrier, inc=1, device_id={"nodes": lax.rem(me + step, size)}, device_id_type=MESH
        )
        return carry

    lax.fori_loop(1, size, greet, 0)

    rows = []
    for number, (start, width, wide) in enumerate(pieces):
        for block in range(owned):
            part = state[block * BLOCK : (block + 1) * BLOCK, start : start + width]
            weight = columns[block * BLOCK : (block + 1) * BLOCK, 0:1]
            row = jnp.sum(part * weight, axis=0, keepdims=True)
            if width < wide:
                part = jnp.concatenate([part, jnp.zeros((BLOCK, wide - width), jnp.float32)], 1)
            if width < PIECE:
                row = jnp.concatenate([row, jnp.zeros((1, PIECE - width), jnp.float32)], 1)
            ext[number][block] = part.astype(jnp.bfloat16)
            rows.append(row)
    pooled[me] = jnp.concatenate(rows, 0).astype(jnp.bfloat16)

    pl.semaphore_wait(barrier, size - 1)

    def block_copy(number, kind, source, target):
        return pltpu.make_async_remote_copy(
            src_ref=ext[number].at[pl.ds(source * owned, owned)],
            dst_ref=ext[number].at[pl.ds((kind + 1) * owned, owned)],
            send_sem=own_send.at[number, kind],
            recv_sem=own_recv.at[number, kind],
            device_id={"nodes": target},
            device_id_type=MESH,
        )

    relayed = jnp.where(core == odd, 2, 3)
    to_mate = [block_copy(n, 0, 0, mate) for n in range(count)]
    to_partner = [block_copy(n, 1, 0, partner) for n in range(count)]
    forward = [block_copy(n, 2, 2, onward) for n in range(count)]
    relay = [block_copy(n, 3, relayed, mate) for n in range(count)]

    to_partner[0].start()
    list_copies = []
    for column, offset in enumerate((1, -1, 2, -2)):
        copy = pltpu.make_async_remote_copy(
            src_ref=list_ref,
            dst_ref=lists.at[column],
            send_sem=list_send.at[column],
            recv_sem=list_recv.at[column],
            device_id={"nodes": lax.rem(me + offset + size, size)},
            device_id_type=MESH,
        )
        copy.start()
        list_copies.append(copy)

    def pool_copy(step):
        return pltpu.make_async_remote_copy(
            src_ref=pooled.at[me],
            dst_ref=pooled.at[me],
            send_sem=pool_send.at[step],
            recv_sem=pool_recv.at[step],
            device_id={"nodes": lax.rem(me + step, size)},
            device_id_type=MESH,
        )

    def pool_arrival(step):
        return pltpu.make_async_remote_copy(
            src_ref=pooled.at[me],
            dst_ref=pooled.at[lax.rem(me - step + size, size)],
            send_sem=pool_send.at[step],
            recv_sem=pool_recv.at[step],
            device_id={"nodes": lax.rem(me + step, size)},
            device_id_type=MESH,
        )

    def send_pooled(step, carry):
        pool_copy(step).start()
        return carry

    lax.fori_loop(1, size, send_pooled, 0)
    for copy in to_partner[1:] + to_mate:
        copy.start()

    live = edge_count[0]

    def panel(slot, carry):
        block = matrix[slot]
        at = pl.ds(pl.multiple_of(slot * BLOCK, BLOCK), BLOCK)
        for owner in range(owned):
            use = jnp.where((edge_dst[0, slot] == owner) & (slot < live), 1.0, 0.0)
            weights[owner * BLOCK : (owner + 1) * BLOCK, at] = (block * use).astype(jnp.bfloat16)
        return carry

    lax.fori_loop(0, slots, panel, 0)

    for copy in list_copies:
        copy.wait()
    to_scalar = pltpu.make_async_copy(lists, lists_scalar, local_sem)
    to_scalar.start()
    to_scalar.wait()

    behind_one = jnp.where(core == 1, 1, 4)
    ahead_one = jnp.where(core == 0, 1, 4)
    behind_two = jnp.where(odd == 0, 3, 2)
    ahead_two = jnp.where(odd == 0, 2, 3)

    def place(slot):
        source = edge_src[0, slot]
        away = jnp.maximum(source - owned, 0)
        column = away // 2
        base = jnp.where(
            column == 0,
            behind_one,
            jnp.where(column == 1, ahead_one, jnp.where(column == 2, behind_two, ahead_two)),
        )
        block = lists_scalar[column, 0, away]
        return jnp.where(source < owned, source, base * owned + block)

    def wait_pooled(step, carry):
        pool_arrival(step).wait()
        return carry

    def combine(number):
        start, width, wide = pieces[number]
        buffer = ext[number]

        def pick(slot, carry):
            at = pl.ds(pl.multiple_of(slot * BLOCK, BLOCK), BLOCK)
            gathered[at, :wide] = buffer[place(slot)]
            return carry

        lax.fori_loop(0, slots, pick, 0)
        if number == 0:
            lax.fori_loop(1, size, wait_pooled, 0)
        every = pooled[...].reshape(-1, PIECE)
        mixed = jnp.dot(mixing[number], every, preferred_element_type=jnp.float32)
        for owner in range(owned):
            coarse[owner] = jnp.broadcast_to(mixed[owner : owner + 1], (8, PIECE))

        def rows_of(owner, carry):
            at = pl.ds(pl.multiple_of(owner * BLOCK, BLOCK), BLOCK)
            moved = jnp.dot(
                weights[at, :], gathered[:, :wide], preferred_element_type=jnp.float32
            )
            lifted = columns[at, 1:2] * coarse[owner][0:1, :width]
            field[at, start : start + width] = (
                state[at, start : start + width] + moved[:, :width] + lifted
            )
            return carry

        lax.fori_loop(0, owned, rows_of, 0)

    for number in range(count + 1):
        if number < count:
            to_partner[number].wait()
            forward[number].start()
        if number >= 1:
            forward[number - 1].wait()
            relay[number - 1].start()
            to_mate[number - 1].wait()
            relay[number - 1].wait()
            combine(number - 1)


def network_kernel(field, gain, proj_in, proj_out, out):
    flat = field[...]
    mean_square = jnp.mean(flat * flat, axis=1, keepdims=True)
    normed = (flat * lax.rsqrt(mean_square + 1e-06) * gain[...]).astype(jnp.bfloat16)
    pre_act = jnp.dot(normed, proj_in[...], preferred_element_type=jnp.float32)
    hidden = jax.nn.gelu(pre_act).astype(jnp.bfloat16)
    out[...] = flat + jnp.dot(hidden, proj_out[...], preferred_element_type=jnp.float32)


def shards(
    size,
    wave_state,
    pool_weight,
    lift_weight,
    coarse_matrix,
    block_matrix,
    edge_dst,
    edge_src,
    edge_count,
    send_list,
    norm_gain,
    proj_in,
    proj_out,
):
    nodes, bins = wave_state.shape
    owned = nodes // BLOCK
    slots = edge_src.shape[1]
    pieces = pieces_of(bins)
    count = len(pieces)
    position = lax.axis_index("nodes")
    mine = lax.dynamic_slice_in_dim(coarse_matrix, position * owned, owned, 0)
    mine = mine.reshape(1, owned, size, 1, owned)
    same = jnp.eye(count, dtype=jnp.bfloat16).reshape(count, 1, 1, count, 1)
    mixing = (mine * same).reshape(count, owned, size * count * owned)
    mixing = jnp.pad(mixing, ((0, 0), (0, 16 - owned), (0, 0)))
    columns = jnp.stack([pool_weight, lift_weight], axis=1)
    lists = jnp.pad(send_list.reshape(1, -1), ((0, 7), (0, 120)))

    vmem = pl.BlockSpec(memory_space=pltpu.VMEM)
    smem = pl.BlockSpec(memory_space=pltpu.SMEM)
    field = pl.pallas_call(
        functools.partial(exchange_kernel, size, owned, pieces),
        out_shape=jax.ShapeDtypeStruct((nodes, bins), jnp.float32),
        in_specs=[vmem, vmem, vmem, vmem, smem, smem, smem, vmem],
        out_specs=vmem,
        scratch_shapes=[
            pltpu.VMEM((nodes, slots * BLOCK), jnp.bfloat16),
            pltpu.VMEM((slots * BLOCK, PIECE), jnp.bfloat16),
            pltpu.VMEM((size, count * owned, PIECE), jnp.bfloat16),
            pltpu.VMEM((4, 8, 128), jnp.int32),
            pltpu.SMEM((4, 8, 128), jnp.int32),
            pltpu.VMEM((owned, 8, PIECE), jnp.float32),
            pltpu.SemaphoreType.DMA((count, 4)),
            pltpu.SemaphoreType.DMA((count, 4)),
            pltpu.SemaphoreType.DMA((4,)),
            pltpu.SemaphoreType.DMA((4,)),
            pltpu.SemaphoreType.DMA((size,)),
            pltpu.SemaphoreType.DMA((size,)),
            pltpu.SemaphoreType.DMA,
        ]
        + [pltpu.VMEM((5 * owned, BLOCK, wide), jnp.bfloat16) for _, _, wide in pieces],
        compiler_params=pltpu.CompilerParams(
            collective_id=0, has_side_effects=True, vmem_limit_bytes=40 * 2**20
        ),
        name="exchange",
    )(wave_state, columns, mixing, block_matrix[0], edge_dst, edge_src, edge_count, lists)

    tile = min(256, nodes)
    hidden_size = proj_in.shape[1]
    return pl.pallas_call(
        network_kernel,
        grid=(nodes // tile,),
        out_shape=jax.ShapeDtypeStruct((nodes, bins), jnp.float32),
        in_specs=[
            pl.BlockSpec((tile, bins), lambda i: (i, 0)),
            pl.BlockSpec((1, bins), lambda i: (0, 0)),
            pl.BlockSpec((bins, hidden_size), lambda i: (0, 0)),
            pl.BlockSpec((hidden_size, bins), lambda i: (0, 0)),
        ],
        out_specs=pl.BlockSpec((tile, bins), lambda i: (i, 0)),
        compiler_params=pltpu.CompilerParams(vmem_limit_bytes=40 * 2**20),
        name="network",
    )(field, norm_gain.reshape(1, bins), proj_in, proj_out)


def solution(mesh):
    in_specs = (
        P(("members", "nodes"), None),
        P("nodes"),
        P("nodes"),
        P(),
        P("nodes", None, None, None),
        P("nodes", None),
        P("nodes", None),
        P("nodes"),
        P("nodes", None, None),
        P(),
        P(),
        P(),
    )
    out_specs = P(("members", "nodes"), None)
    return jax.shard_map(
        functools.partial(shards, mesh.shape["nodes"]),
        mesh=mesh,
        in_specs=in_specs,
        out_specs=out_specs,
        check_vma=False,
    )
```

```python
import functools

import jax
import jax.numpy as jnp
from jax import lax
from jax.experimental import pallas as pl
from jax.experimental.pallas import tpu as pltpu
from jax.sharding import PartitionSpec as P

BLOCK = 128
PIECE = 384
CHUNK = 144
MESH = pl.DeviceIdType.MESH


def exchange_kernel(
    size, owned, chunk, pieces,
    state, pool, lift, mixing, matrix, edge_dst, edge_src, edge_count, list_ref, gain_row, proj_in_hbm, proj_out_hbm,
    out,
    weights, gathered, pooled, lists, lists_scalar, coarse, gain, proj_in, proj_in_turned, proj_out,
    own_send, own_recv, list_send, list_recv, pool_send, pool_recv, local_sem,
    *ext,
):
    bins, nodes = state.shape
    slots = matrix.shape[0]
    count = len(ext)
    me = lax.axis_index("nodes")
    core = lax.rem(me, 2)
    chip = me // 2
    odd = lax.rem(chip, 2)
    mate = chip * 2 + 1 - core
    partner = (chip + 1 - 2 * odd) * 2 + core
    onward = lax.rem(me + 4 - 8 * odd + size, size)

    barrier = pltpu.get_barrier_semaphore()

    def greet(step, carry):
        pl.semaphore_signal(
            barrier, inc=1, device_id={"nodes": lax.rem(me + step, size)}, device_id_type=MESH
        )
        return carry

    lax.fori_loop(1, size, greet, 0)
    fetch_in = pltpu.make_async_copy(proj_in_hbm, proj_in, local_sem.at[1])
    fetch_out = pltpu.make_async_copy(proj_out_hbm, proj_out, local_sem.at[2])
    fetch_in.start()
    fetch_out.start()

    for number in range(count):
        for block in range(owned):
            part = state[number * chunk : (number + 1) * chunk, block * BLOCK : (block + 1) * BLOCK]
            ext[number][block] = part.astype(jnp.bfloat16)

    pl.semaphore_wait(barrier, size - 1)

    def block_copy(number, kind, source, target):
        return pltpu.make_async_remote_copy(
            src_ref=ext[number].at[pl.ds(source * owned, owned)],
            dst_ref=ext[number].at[pl.ds((kind + 1) * owned, owned)],
            send_sem=own_send.at[number, kind],
            recv_sem=own_recv.at[number, kind],
            device_id={"nodes": target},
            device_id_type=MESH,
        )

    relayed = jnp.where(core == odd, 2, 3)
    to_mate = [block_copy(n, 0, 0, mate) for n in range(count)]
    to_partner = [block_copy(n, 1, 0, partner) for n in range(count)]
    forward = [block_copy(n, 2, 2, onward) for n in range(count)]
    relay = [block_copy(n, 3, relayed, mate) for n in range(count)]

    to_partner[0].start()
    to_partner[1].start()
    list_copies = []
    for column, offset in enumerate((1, -1, 2, -2)):
        copy = pltpu.make_async_remote_copy(
            src_ref=list_ref,
            dst_ref=lists.at[column],
            send_sem=list_send.at[column],
            recv_sem=list_recv.at[column],
            device_id={"nodes": lax.rem(me + offset + size, size)},
            device_id_type=MESH,
        )
        copy.start()
        list_copies.append(copy)

    row_id = lax.broadcasted_iota(jnp.int32, (16, nodes), 0)
    node_block = lax.broadcasted_iota(jnp.int32, (16, nodes), 1) // BLOCK
    pooling = jnp.where(row_id == node_block, jnp.broadcast_to(pool[...], (16, nodes)), 0.0)
    rows = []
    for start, width in pieces:
        part = lax.dot_general(
            pooling,
            state[start : start + width, :],
            (((1,), (1,)), ((), ())),
            precision=lax.Precision.HIGHEST,
            preferred_element_type=jnp.float32,
        )[:owned]
        if width < PIECE:
            part = jnp.concatenate([part, jnp.zeros((owned, PIECE - width), jnp.float32)], 1)
        rows.append(part)
    pooled[me] = jnp.concatenate(rows, 0).astype(jnp.bfloat16)

    def pool_copy(step, row):
        return pltpu.make_async_remote_copy(
            src_ref=pooled.at[me],
            dst_ref=pooled.at[row],
            send_sem=pool_send.at[step],
            recv_sem=pool_recv.at[step],
            device_id={"nodes": lax.rem(me + step, size)},
            device_id_type=MESH,
        )

    def send_pooled(step, carry):
        pool_copy(step, me).start()
        return carry

    lax.fori_loop(1, size, send_pooled, 0)
    for copy in to_partner[2:] + to_mate:
        copy.start()

    live = edge_count[0]

    def panel(slot, carry):
        block = matrix[slot].T
        at = pl.ds(pl.multiple_of(slot * BLOCK, BLOCK), BLOCK)
        for owner in range(owned):
            use = jnp.where((edge_dst[0, slot] == owner) & (slot < live), 1.0, 0.0)
            weights[at, owner * BLOCK : (owner + 1) * BLOCK] = (block * use).astype(jnp.bfloat16)
        return carry

    lax.fori_loop(0, slots, panel, 0)

    for copy in list_copies:
        copy.wait()
    to_scalar = pltpu.make_async_copy(lists, lists_scalar, local_sem.at[0])
    to_scalar.start()
    to_scalar.wait()

    behind_one = jnp.where(core == 1, 1, 4)
    ahead_one = jnp.where(core == 0, 1, 4)
    behind_two = jnp.where(odd == 0, 3, 2)
    ahead_two = jnp.where(odd == 0, 2, 3)

    def place(slot):
        source = edge_src[0, slot]
        away = jnp.maximum(source - owned, 0)
        column = away // 2
        base = jnp.where(
            column == 0,
            behind_one,
            jnp.where(column == 1, ahead_one, jnp.where(column == 2, behind_two, ahead_two)),
        )
        block = lists_scalar[column, 0, away]
        return jnp.where(source < owned, source, base * owned + block)

    def wait_pooled(step, carry):
        pool_copy(step, lax.rem(me - step + size, size)).wait()
        return carry

    def mix():
        lax.fori_loop(1, size, wait_pooled, 0)
        every = pooled[...].reshape(-1, PIECE)
        for number, (start, width) in enumerate(pieces):
            mixed = jnp.dot(mixing[number], every, preferred_element_type=jnp.float32)
            mixed = jnp.concatenate([mixed, jnp.zeros((BLOCK - 16, PIECE), jnp.float32)], 0)
            coarse[start : start + width, :] = mixed.T[:width]

    def turn():
        spread = jnp.broadcast_to(gain_row[...], (BLOCK, gain_row.shape[1]))
        gain[...] = spread.T[:bins]
        fetch_in.wait()
        for at in range(0, proj_in.shape[1], BLOCK):
            proj_in_turned[at : at + BLOCK, :] = proj_in[:, at : at + BLOCK].T

    def combine(number):
        buffer = ext[number]
        at_bins = slice(number * chunk, (number + 1) * chunk)

        def pick(slot, carry):
            at = pl.ds(pl.multiple_of(slot * BLOCK, BLOCK), BLOCK)
            gathered[:, at] = buffer[place(slot)]
            return carry

        lax.fori_loop(0, slots, pick, 0)
        moved = jnp.dot(gathered[...], weights[...], preferred_element_type=jnp.float32)
        for owner in range(owned):
            own = slice(owner * BLOCK, (owner + 1) * BLOCK)
            lifted = coarse[at_bins, owner : owner + 1] * lift[0:1, own]
            out[at_bins, own] = state[at_bins, own] + moved[:, own] + lifted

    for number in range(count + 2):
        if number < count:
            to_partner[number].wait()
            forward[number].start()
        if 1 <= number <= count:
            forward[number - 1].wait()
            relay[number - 1].start()
        if number == 1:
            mix()
            turn()
        if number >= 2:
            to_mate[number - 2].wait()
            relay[number - 2].wait()
            combine(number - 2)

    fetch_out.wait()
    tile = 2 * BLOCK

    def network(step, carry):
        at = pl.ds(pl.multiple_of(step * tile, tile), tile)
        flat = out[:, at]
        mean_square = jnp.mean(flat * flat, axis=0, keepdims=True)
        wide_gain = jnp.concatenate([gain[...]] * 2, 1)
        normed = (flat * lax.rsqrt(mean_square + 1e-06) * wide_gain).astype(jnp.bfloat16)
        pre_act = jnp.dot(proj_in_turned[...], normed, preferred_element_type=jnp.float32)
        hidden = jax.nn.gelu(pre_act).astype(jnp.bfloat16)
        out[:, at] = out[:, at] + jnp.dot(proj_out[...], hidden, preferred_element_type=jnp.float32)
        return carry

    lax.fori_loop(0, nodes // tile, network, 0)


def shards(
    size,
    wave_state,
    pool_weight,
    lift_weight,
    coarse_matrix,
    block_matrix,
    edge_dst,
    edge_src,
    edge_count,
    send_list,
    norm_gain,
    proj_in,
    proj_out,
):
    nodes, bins = wave_state.shape
    owned = nodes // BLOCK
    slots = edge_src.shape[1]
    hidden_size = proj_in.shape[1]
    pieces = [(start, min(PIECE, bins - start)) for start in range(0, bins, PIECE)]
    count = len(pieces)
    chunk = CHUNK
    chunks = bins // chunk
    position = lax.axis_index("nodes")
    mine = lax.dynamic_slice_in_dim(coarse_matrix, position * owned, owned, 0)
    mine = mine.reshape(1, owned, size, 1, owned)
    same = jnp.eye(count, dtype=jnp.bfloat16).reshape(count, 1, 1, count, 1)
    mixing = (mine * same).reshape(count, owned, size * count * owned)
    mixing = jnp.pad(mixing, ((0, 0), (0, 16 - owned), (0, 0)))
    lists = jnp.pad(send_list.reshape(1, -1), ((0, 7), (0, 120)))
    gain_row = jnp.pad(norm_gain, (0, -bins % BLOCK)).reshape(1, -1)

    vmem = pl.BlockSpec(memory_space=pltpu.VMEM)
    smem = pl.BlockSpec(memory_space=pltpu.SMEM)
    anywhere = pl.BlockSpec(memory_space=pl.ANY)
    turned = pl.pallas_call(
        functools.partial(exchange_kernel, size, owned, chunk, pieces),
        out_shape=jax.ShapeDtypeStruct((bins, nodes), jnp.float32),
        in_specs=[vmem] * 5 + [smem] * 3 + [vmem] * 2 + [anywhere] * 2,
        out_specs=vmem,
        scratch_shapes=[
            pltpu.VMEM((slots * BLOCK, nodes), jnp.bfloat16),
            pltpu.VMEM((chunk, slots * BLOCK), jnp.bfloat16),
            pltpu.VMEM((size, count * owned, PIECE), jnp.bfloat16),
            pltpu.VMEM((4, 8, 128), jnp.int32),
            pltpu.SMEM((4, 8, 128), jnp.int32),
            pltpu.VMEM((bins, BLOCK), jnp.float32),
            pltpu.VMEM((bins, BLOCK), jnp.float32),
            pltpu.VMEM((bins, hidden_size), jnp.bfloat16),
            pltpu.VMEM((hidden_size, bins), jnp.bfloat16),
            pltpu.VMEM((bins, hidden_size), jnp.bfloat16),
            pltpu.SemaphoreType.DMA((chunks, 4)),
            pltpu.SemaphoreType.DMA((chunks, 4)),
            pltpu.SemaphoreType.DMA((4,)),
            pltpu.SemaphoreType.DMA((4,)),
            pltpu.SemaphoreType.DMA((size,)),
            pltpu.SemaphoreType.DMA((size,)),
            pltpu.SemaphoreType.DMA((3,)),
        ]
        + [pltpu.VMEM((5 * owned, chunk, BLOCK), jnp.bfloat16)] * chunks,
        compiler_params=pltpu.CompilerParams(
            collective_id=0, has_side_effects=True, vmem_limit_bytes=48 * 2**20
        ),
        name="exchange",
    )(
        wave_state.T,
        pool_weight.reshape(1, nodes),
        lift_weight.reshape(1, nodes),
        mixing,
        block_matrix[0],
        edge_dst,
        edge_src,
        edge_count,
        lists,
        gain_row,
        proj_in,
        proj_out.T,
    )
    return turned.T


def solution(mesh):
    in_specs = (
        P(("members", "nodes"), None),
        P("nodes"),
        P("nodes"),
        P(),
        P("nodes", None, None, None),
        P("nodes", None),
        P("nodes", None),
        P("nodes"),
        P("nodes", None, None),
        P(),
        P(),
        P(),
    )
    out_specs = P(("members", "nodes"), None)
    return jax.shard_map(
        functools.partial(shards, mesh.shape["nodes"]),
        mesh=mesh,
        in_specs=in_specs,
        out_specs=out_specs,
        check_vma=False,
    )
```

```python
import functools

import jax
import jax.numpy as jnp
from jax import lax
from jax.experimental import pallas as pl
from jax.experimental.pallas import tpu as pltpu
from jax.sharding import PartitionSpec as P

BLOCK = 128
PIECE = 384
CHUNK = 144
MESH = pl.DeviceIdType.MESH


def exchange_kernel(
    size, owned, chunk, pieces,
    state, pool_hbm, lift_hbm, mixing, matrix_hbm, edge_dst_hbm, edge_src_hbm, edge_count, list_ref, gain_row,
    proj_in_hbm, proj_out_hbm,
    out,
    pool, lift, matrix, edge_dst, edge_src,
    weights, gathered, pooled, lists, lists_scalar, coarse, gain, proj_in, proj_in_turned, proj_out,
    own_send, own_recv, list_send, list_recv, pool_send, pool_recv, local_sem,
    *ext,
):
    bins, nodes = state.shape
    slots = matrix.shape[0]
    count = len(ext)
    me = lax.axis_index("nodes")
    core = lax.rem(me, 2)
    chip = me // 2
    odd = lax.rem(chip, 2)
    mate = chip * 2 + 1 - core
    partner = (chip + 1 - 2 * odd) * 2 + core
    onward = lax.rem(me + 4 - 8 * odd + size, size)

    barrier = pltpu.get_barrier_semaphore()

    def greet(step, carry):
        pl.semaphore_signal(
            barrier, inc=1, device_id={"nodes": lax.rem(me + step, size)}, device_id_type=MESH
        )
        return carry

    lax.fori_loop(1, size, greet, 0)
    fetch_in = pltpu.make_async_copy(proj_in_hbm, proj_in, local_sem.at[1])
    fetch_out = pltpu.make_async_copy(proj_out_hbm, proj_out, local_sem.at[2])
    fetch_small = [
        pltpu.make_async_copy(source, target, local_sem.at[3 + number])
        for number, (source, target) in enumerate(
            [
                (pool_hbm, pool),
                (lift_hbm, lift),
                (edge_dst_hbm, edge_dst),
                (edge_src_hbm, edge_src),
                (matrix_hbm, matrix),
            ]
        )
    ]
    for copy in fetch_small + [fetch_in, fetch_out]:
        copy.start()

    for number in range(count):
        for block in range(owned):
            part = state[number * chunk : (number + 1) * chunk, block * BLOCK : (block + 1) * BLOCK]
            ext[number][block] = part.astype(jnp.bfloat16)

    pl.semaphore_wait(barrier, size - 1)

    def block_copy(number, kind, source, target):
        return pltpu.make_async_remote_copy(
            src_ref=ext[number].at[pl.ds(source * owned, owned)],
            dst_ref=ext[number].at[pl.ds((kind + 1) * owned, owned)],
            send_sem=own_send.at[number, kind],
            recv_sem=own_recv.at[number, kind],
            device_id={"nodes": target},
            device_id_type=MESH,
        )

    relayed = jnp.where(core == odd, 2, 3)
    to_mate = [block_copy(n, 0, 0, mate) for n in range(count)]
    to_partner = [block_copy(n, 1, 0, partner) for n in range(count)]
    forward = [block_copy(n, 2, 2, onward) for n in range(count)]
    relay = [block_copy(n, 3, relayed, mate) for n in range(count)]

    to_partner[0].start()
    to_partner[1].start()
    list_copies = []
    for column, offset in enumerate((1, -1, 2, -2)):
        copy = pltpu.make_async_remote_copy(
            src_ref=list_ref,
            dst_ref=lists.at[column],
            send_sem=list_send.at[column],
            recv_sem=list_recv.at[column],
            device_id={"nodes": lax.rem(me + offset + size, size)},
            device_id_type=MESH,
        )
        copy.start()
        list_copies.append(copy)

    for copy in fetch_small:
        copy.wait()

    row_id = lax.broadcasted_iota(jnp.int32, (16, nodes), 0)
    node_block = lax.broadcasted_iota(jnp.int32, (16, nodes), 1) // BLOCK
    pooling = jnp.where(row_id == node_block, jnp.broadcast_to(pool[...], (16, nodes)), 0.0)
    rows = []
    for start, width in pieces:
        part = lax.dot_general(
            pooling,
            state[start : start + width, :],
            (((1,), (1,)), ((), ())),
            precision=lax.Precision.HIGHEST,
            preferred_element_type=jnp.float32,
        )[:owned]
        if width < PIECE:
            part = jnp.concatenate([part, jnp.zeros((owned, PIECE - width), jnp.float32)], 1)
        rows.append(part)
    pooled[me] = jnp.concatenate(rows, 0).astype(jnp.bfloat16)

    def pool_copy(step, row):
        return pltpu.make_async_remote_copy(
            src_ref=pooled.at[me],
            dst_ref=pooled.at[row],
            send_sem=pool_send.at[step],
            recv_sem=pool_recv.at[step],
            device_id={"nodes": lax.rem(me + step, size)},
            device_id_type=MESH,
        )

    def send_pooled(step, carry):
        pool_copy(step, me).start()
        return carry

    lax.fori_loop(1, size, send_pooled, 0)
    for copy in to_partner[2:] + to_mate:
        copy.start()

    live = edge_count[0]

    def panel(slot, carry):
        block = matrix[slot].T
        at = pl.ds(pl.multiple_of(slot * BLOCK, BLOCK), BLOCK)
        for owner in range(owned):
            use = jnp.where((edge_dst[0, slot] == owner) & (slot < live), 1.0, 0.0)
            weights[at, owner * BLOCK : (owner + 1) * BLOCK] = (block * use).astype(jnp.bfloat16)
        return carry

    lax.fori_loop(0, slots, panel, 0)

    for copy in list_copies:
        copy.wait()
    to_scalar = pltpu.make_async_copy(lists, lists_scalar, local_sem.at[0])
    to_scalar.start()
    to_scalar.wait()

    behind_one = jnp.where(core == 1, 1, 4)
    ahead_one = jnp.where(core == 0, 1, 4)
    behind_two = jnp.where(odd == 0, 3, 2)
    ahead_two = jnp.where(odd == 0, 2, 3)

    def place(slot):
        source = edge_src[0, slot]
        away = jnp.maximum(source - owned, 0)
        column = away // 2
        base = jnp.where(
            column == 0,
            behind_one,
            jnp.where(column == 1, ahead_one, jnp.where(column == 2, behind_two, ahead_two)),
        )
        block = lists_scalar[column, 0, away]
        return jnp.where(source < owned, source, base * owned + block)

    def wait_pooled(step, carry):
        pool_copy(step, lax.rem(me - step + size, size)).wait()
        return carry

    def mix():
        lax.fori_loop(1, size, wait_pooled, 0)
        every = pooled[...].reshape(-1, PIECE)
        for number, (start, width) in enumerate(pieces):
            mixed = jnp.dot(mixing[number], every, preferred_element_type=jnp.float32)
            mixed = jnp.concatenate([mixed, jnp.zeros((BLOCK - 16, PIECE), jnp.float32)], 0)
            coarse[start : start + width, :] = mixed.T[:width]

    def turn_gain():
        spread = jnp.broadcast_to(gain_row[...], (BLOCK, gain_row.shape[1]))
        gain[...] = spread.T[:bins]

    def turn(part):
        at = slice(part * BLOCK, (part + 1) * BLOCK)
        proj_in_turned[at, :] = proj_in[:, at].T

    parts = proj_in.shape[1] // BLOCK

    def combine(number):
        buffer = ext[number]
        at_bins = slice(number * chunk, (number + 1) * chunk)

        def pick(slot, carry):
            at = pl.ds(pl.multiple_of(slot * BLOCK, BLOCK), BLOCK)
            gathered[:, at] = buffer[place(slot)]
            return carry

        lax.fori_loop(0, slots, pick, 0)
        moved = jnp.dot(gathered[...], weights[...], preferred_element_type=jnp.float32)
        for owner in range(owned):
            own = slice(owner * BLOCK, (owner + 1) * BLOCK)
            lifted = coarse[at_bins, owner : owner + 1] * lift[0:1, own]
            out[at_bins, own] = state[at_bins, own] + moved[:, own] + lifted

    for number in range(count + 2):
        if number < count:
            to_partner[number].wait()
            forward[number].start()
        if 1 <= number <= count:
            forward[number - 1].wait()
            relay[number - 1].start()
        if number == 1:
            mix()
            turn_gain()
            fetch_in.wait()
        if number >= 2:
            to_mate[number - 2].wait()
            relay[number - 2].wait()
            combine(number - 2)
            for part in range((number - 2) * parts // count, (number - 1) * parts // count):
                turn(part)

    fetch_out.wait()
    tile = 2 * BLOCK

    def network(step, carry):
        at = pl.ds(pl.multiple_of(step * tile, tile), tile)
        flat = out[:, at]
        mean_square = jnp.mean(flat * flat, axis=0, keepdims=True)
        wide_gain = jnp.concatenate([gain[...]] * 2, 1)
        normed = (flat * lax.rsqrt(mean_square + 1e-06) * wide_gain).astype(jnp.bfloat16)
        pre_act = jnp.dot(proj_in_turned[...], normed, preferred_element_type=jnp.float32)
        hidden = jax.nn.gelu(pre_act).astype(jnp.bfloat16)
        out[:, at] = out[:, at] + jnp.dot(proj_out[...], hidden, preferred_element_type=jnp.float32)
        return carry

    lax.fori_loop(0, nodes // tile, network, 0)


def shards(
    size,
    wave_state,
    pool_weight,
    lift_weight,
    coarse_matrix,
    block_matrix,
    edge_dst,
    edge_src,
    edge_count,
    send_list,
    norm_gain,
    proj_in,
    proj_out,
):
    nodes, bins = wave_state.shape
    owned = nodes // BLOCK
    slots = edge_src.shape[1]
    hidden_size = proj_in.shape[1]
    pieces = [(start, min(PIECE, bins - start)) for start in range(0, bins, PIECE)]
    count = len(pieces)
    chunk = CHUNK
    chunks = bins // chunk
    position = lax.axis_index("nodes")
    mine = lax.dynamic_slice_in_dim(coarse_matrix, position * owned, owned, 0)
    mine = mine.reshape(1, owned, size, 1, owned)
    same = jnp.eye(count, dtype=jnp.bfloat16).reshape(count, 1, 1, count, 1)
    mixing = (mine * same).reshape(count, owned, size * count * owned)
    mixing = jnp.pad(mixing, ((0, 0), (0, 16 - owned), (0, 0)))
    lists = jnp.pad(send_list.reshape(1, -1), ((0, 7), (0, 120)))
    gain_row = jnp.pad(norm_gain, (0, -bins % BLOCK)).reshape(1, -1)

    vmem = pl.BlockSpec(memory_space=pltpu.VMEM)
    smem = pl.BlockSpec(memory_space=pltpu.SMEM)
    anywhere = pl.BlockSpec(memory_space=pl.ANY)
    turned = pl.pallas_call(
        functools.partial(exchange_kernel, size, owned, chunk, pieces),
        out_shape=jax.ShapeDtypeStruct((bins, nodes), jnp.float32),
        in_specs=[vmem, anywhere, anywhere, vmem]
        + [anywhere] * 3
        + [smem]
        + [vmem] * 2
        + [anywhere] * 2,
        out_specs=vmem,
        scratch_shapes=[
            pltpu.VMEM((1, nodes), jnp.float32),
            pltpu.VMEM((1, nodes), jnp.float32),
            pltpu.VMEM((slots, BLOCK, BLOCK), jnp.float32),
            pltpu.SMEM((1, slots), jnp.int32),
            pltpu.SMEM((1, slots), jnp.int32),
            pltpu.VMEM((slots * BLOCK, nodes), jnp.bfloat16),
            pltpu.VMEM((chunk, slots * BLOCK), jnp.bfloat16),
            pltpu.VMEM((size, count * owned, PIECE), jnp.bfloat16),
            pltpu.VMEM((4, 8, 128), jnp.int32),
            pltpu.SMEM((4, 8, 128), jnp.int32),
            pltpu.VMEM((bins, BLOCK), jnp.float32),
            pltpu.VMEM((bins, BLOCK), jnp.float32),
            pltpu.VMEM((bins, hidden_size), jnp.bfloat16),
            pltpu.VMEM((hidden_size, bins), jnp.bfloat16),
            pltpu.VMEM((bins, hidden_size), jnp.bfloat16),
            pltpu.SemaphoreType.DMA((chunks, 4)),
            pltpu.SemaphoreType.DMA((chunks, 4)),
            pltpu.SemaphoreType.DMA((4,)),
            pltpu.SemaphoreType.DMA((4,)),
            pltpu.SemaphoreType.DMA((size,)),
            pltpu.SemaphoreType.DMA((size,)),
            pltpu.SemaphoreType.DMA((8,)),
        ]
        + [pltpu.VMEM((5 * owned, chunk, BLOCK), jnp.bfloat16)] * chunks,
        compiler_params=pltpu.CompilerParams(
            collective_id=0, has_side_effects=True, vmem_limit_bytes=60 * 2**20
        ),
        name="exchange",
    )(
        wave_state.T,
        pool_weight.reshape(1, nodes),
        lift_weight.reshape(1, nodes),
        mixing,
        block_matrix[0],
        edge_dst,
        edge_src,
        edge_count,
        lists,
        gain_row,
        proj_in,
        proj_out.T,
    )
    return turned.T


def solution(mesh):
    in_specs = (
        P(("members", "nodes"), None),
        P("nodes"),
        P("nodes"),
        P(),
        P("nodes", None, None, None),
        P("nodes", None),
        P("nodes", None),
        P("nodes"),
        P("nodes", None, None),
        P(),
        P(),
        P(),
    )
    out_specs = P(("members", "nodes"), None)
    return jax.shard_map(
        functools.partial(shards, mesh.shape["nodes"]),
        mesh=mesh,
        in_specs=in_specs,
        out_specs=out_specs,
        check_vma=False,
    )
```

```python
import functools

import jax
import jax.numpy as jnp
from jax import lax
from jax.experimental import pallas as pl
from jax.experimental.pallas import tpu as pltpu
from jax.sharding import PartitionSpec as P

BLOCK = 128
PIECE = 384
CHUNK = 144
MESH = pl.DeviceIdType.MESH


def exchange_kernel(
    size, owned, chunk, pieces,
    state, pool_hbm, lift_hbm, mixing, matrix_hbm, edge_dst_hbm, edge_src_hbm, edge_count, list_ref, gain_row,
    proj_in_hbm, proj_out_hbm,
    out,
    pool, lift, matrix, edge_dst, edge_src,
    weights, gathered, pooled, lists, lists_scalar, coarse, gain, proj_in, proj_in_turned, proj_out,
    own_send, own_recv, list_send, list_recv, pool_send, pool_recv, local_sem,
    *ext,
):
    bins, nodes = state.shape
    slots = matrix.shape[0]
    count = len(ext)
    me = lax.axis_index("nodes")
    core = lax.rem(me, 2)
    chip = me // 2
    odd = lax.rem(chip, 2)
    mate = chip * 2 + 1 - core
    partner = (chip + 1 - 2 * odd) * 2 + core
    onward = lax.rem(me + 4 - 8 * odd + size, size)

    barrier = pltpu.get_barrier_semaphore()

    def greet(step, carry):
        pl.semaphore_signal(
            barrier, inc=1, device_id={"nodes": lax.rem(me + step, size)}, device_id_type=MESH
        )
        return carry

    lax.fori_loop(1, size, greet, 0)
    fetch_in = pltpu.make_async_copy(proj_in_hbm, proj_in, local_sem.at[1])
    fetch_out = pltpu.make_async_copy(proj_out_hbm, proj_out, local_sem.at[2])
    fetch_small = [
        pltpu.make_async_copy(source, target, local_sem.at[3 + number])
        for number, (source, target) in enumerate(
            [
                (pool_hbm, pool),
                (lift_hbm, lift),
                (edge_dst_hbm, edge_dst),
                (edge_src_hbm, edge_src),
                (matrix_hbm, matrix),
            ]
        )
    ]
    for copy in fetch_small + [fetch_in, fetch_out]:
        copy.start()

    for number in range(count):
        for block in range(owned):
            part = state[number * chunk : (number + 1) * chunk, block * BLOCK : (block + 1) * BLOCK]
            ext[number][block] = part.astype(jnp.bfloat16)

    pl.semaphore_wait(barrier, size - 1)

    def block_copy(number, kind, source, target):
        return pltpu.make_async_remote_copy(
            src_ref=ext[number].at[pl.ds(source * owned, owned)],
            dst_ref=ext[number].at[pl.ds((kind + 1) * owned, owned)],
            send_sem=own_send.at[number, kind],
            recv_sem=own_recv.at[number, kind],
            device_id={"nodes": target},
            device_id_type=MESH,
        )

    relayed = jnp.where(core == odd, 2, 3)
    to_mate = [block_copy(n, 0, 0, mate) for n in range(count)]
    to_partner = [block_copy(n, 1, 0, partner) for n in range(count)]
    forward = [block_copy(n, 2, 2, onward) for n in range(count)]
    relay = [block_copy(n, 3, relayed, mate) for n in range(count)]

    to_partner[0].start()
    to_partner[1].start()
    list_copies = []
    for column, offset in enumerate((1, -1, 2, -2)):
        copy = pltpu.make_async_remote_copy(
            src_ref=list_ref,
            dst_ref=lists.at[column],
            send_sem=list_send.at[column],
            recv_sem=list_recv.at[column],
            device_id={"nodes": lax.rem(me + offset + size, size)},
            device_id_type=MESH,
        )
        copy.start()
        list_copies.append(copy)

    for copy in fetch_small:
        copy.wait()

    row_id = lax.broadcasted_iota(jnp.int32, (16, nodes), 0)
    node_block = lax.broadcasted_iota(jnp.int32, (16, nodes), 1) // BLOCK
    pooling = jnp.where(row_id == node_block, jnp.broadcast_to(pool[...], (16, nodes)), 0.0)
    rows = []
    for start, width in pieces:
        part = lax.dot_general(
            pooling,
            state[start : start + width, :],
            (((1,), (1,)), ((), ())),
            precision=lax.Precision.HIGHEST,
            preferred_element_type=jnp.float32,
        )[:owned]
        if width < PIECE:
            part = jnp.concatenate([part, jnp.zeros((owned, PIECE - width), jnp.float32)], 1)
        rows.append(part)
    pooled[me] = jnp.concatenate(rows, 0).astype(jnp.bfloat16)

    def pool_copy(step, row):
        return pltpu.make_async_remote_copy(
            src_ref=pooled.at[me],
            dst_ref=pooled.at[row],
            send_sem=pool_send.at[step],
            recv_sem=pool_recv.at[step],
            device_id={"nodes": lax.rem(me + step, size)},
            device_id_type=MESH,
        )

    def send_pooled(step, carry):
        pool_copy(step, me).start()
        return carry

    lax.fori_loop(1, size, send_pooled, 0)
    for copy in to_partner[2:] + to_mate:
        copy.start()

    live = edge_count[0]

    def panel(slot, carry):
        block = matrix[slot].T
        at = pl.ds(pl.multiple_of(slot * BLOCK, BLOCK), BLOCK)
        for owner in range(owned):
            use = jnp.where((edge_dst[0, slot] == owner) & (slot < live), 1.0, 0.0)
            weights[at, owner * BLOCK : (owner + 1) * BLOCK] = (block * use).astype(jnp.bfloat16)
        return carry

    lax.fori_loop(0, slots, panel, 0)

    for copy in list_copies:
        copy.wait()
    to_scalar = pltpu.make_async_copy(lists, lists_scalar, local_sem.at[0])
    to_scalar.start()
    to_scalar.wait()

    behind_one = jnp.where(core == 1, 1, 4)
    ahead_one = jnp.where(core == 0, 1, 4)
    behind_two = jnp.where(odd == 0, 3, 2)
    ahead_two = jnp.where(odd == 0, 2, 3)

    def place(slot):
        source = edge_src[0, slot]
        away = jnp.maximum(source - owned, 0)
        column = away // 2
        base = jnp.where(
            column == 0,
            behind_one,
            jnp.where(column == 1, ahead_one, jnp.where(column == 2, behind_two, ahead_two)),
        )
        block = lists_scalar[column, 0, away]
        return jnp.where(source < owned, source, base * owned + block)

    def wait_pooled(step, carry):
        pool_copy(step, lax.rem(me - step + size, size)).wait()
        return carry

    def mix():
        lax.fori_loop(1, size, wait_pooled, 0)
        every = pooled[...].reshape(-1, PIECE)
        for number, (start, width) in enumerate(pieces):
            mixed = jnp.dot(mixing[number], every, preferred_element_type=jnp.float32)
            mixed = jnp.concatenate([mixed, jnp.zeros((BLOCK - 16, PIECE), jnp.float32)], 0)
            coarse[start : start + width, :] = mixed.T[:width]

    def turn_gain():
        spread = jnp.broadcast_to(gain_row[...], (BLOCK, gain_row.shape[1]))
        gain[...] = spread.T[:bins]

    def turn(part):
        at = slice(part * BLOCK, (part + 1) * BLOCK)
        proj_in_turned[at, :] = proj_in[:, at].T

    parts = proj_in.shape[1] // BLOCK

    def combine(number):
        buffer = ext[number]
        at_bins = slice(number * chunk, (number + 1) * chunk)

        def pick(slot, carry):
            at = pl.ds(pl.multiple_of(slot * BLOCK, BLOCK), BLOCK)
            gathered[:, at] = buffer[place(slot)]
            return carry

        lax.fori_loop(0, slots, pick, 0)
        moved = jnp.dot(gathered[...], weights[...], preferred_element_type=jnp.float32)
        for owner in range(owned):
            own = slice(owner * BLOCK, (owner + 1) * BLOCK)
            lifted = coarse[at_bins, owner : owner + 1] * lift[0:1, own]
            out[at_bins, own] = state[at_bins, own] + moved[:, own] + lifted

    for number in range(count + 2):
        if number < count:
            to_partner[number].wait()
            forward[number].start()
        if 1 <= number <= count:
            forward[number - 1].wait()
            relay[number - 1].start()
        if number == 1:
            mix()
            turn_gain()
            fetch_in.wait()
        if number >= 2:
            to_mate[number - 2].wait()
            relay[number - 2].wait()
            combine(number - 2)
            for part in range((number - 2) * parts // count, (number - 1) * parts // count):
                turn(part)

    fetch_out.wait()
    tile = 2 * BLOCK

    def network(step, carry):
        at = pl.ds(pl.multiple_of(step * tile, tile), tile)
        flat = out[:, at]
        mean_square = jnp.mean(flat * flat, axis=0, keepdims=True)
        wide_gain = jnp.concatenate([gain[...]] * 2, 1)
        normed = (flat * lax.rsqrt(mean_square + 1e-06) * wide_gain).astype(jnp.bfloat16)
        pre_act = jnp.dot(proj_in_turned[...], normed, preferred_element_type=jnp.float32)
        hidden = jax.nn.gelu(pre_act).astype(jnp.bfloat16)
        out[:, at] = out[:, at] + jnp.dot(proj_out[...], hidden, preferred_element_type=jnp.float32)
        return carry

    lax.fori_loop(0, nodes // tile, network, 0)


def shards(
    size,
    wave_state,
    pool_weight,
    lift_weight,
    coarse_matrix,
    block_matrix,
    edge_dst,
    edge_src,
    edge_count,
    send_list,
    norm_gain,
    proj_in,
    proj_out,
):
    nodes, bins = wave_state.shape
    owned = nodes // BLOCK
    slots = edge_src.shape[1]
    hidden_size = proj_in.shape[1]
    pieces = [(start, min(PIECE, bins - start)) for start in range(0, bins, PIECE)]
    count = len(pieces)
    chunk = CHUNK
    chunks = bins // chunk
    position = lax.axis_index("nodes")
    mine = lax.dynamic_slice_in_dim(coarse_matrix, position * owned, owned, 0)
    mine = mine.reshape(1, owned, size, 1, owned)
    same = jnp.eye(count, dtype=jnp.bfloat16).reshape(count, 1, 1, count, 1)
    mixing = (mine * same).reshape(count, owned, size * count * owned)
    mixing = jnp.pad(mixing, ((0, 0), (0, 16 - owned), (0, 0)))
    lists = jnp.pad(send_list.reshape(1, -1), ((0, 7), (0, 120)))
    gain_row = jnp.pad(norm_gain, (0, -bins % BLOCK)).reshape(1, -1)

    vmem = pl.BlockSpec(memory_space=pltpu.VMEM)
    smem = pl.BlockSpec(memory_space=pltpu.SMEM)
    anywhere = pl.BlockSpec(memory_space=pl.ANY)
    turned = pl.pallas_call(
        functools.partial(exchange_kernel, size, owned, chunk, pieces),
        out_shape=jax.ShapeDtypeStruct((bins, nodes), jnp.float32),
        in_specs=[vmem, anywhere, anywhere, vmem]
        + [anywhere] * 3
        + [smem]
        + [vmem] * 2
        + [anywhere] * 2,
        out_specs=vmem,
        scratch_shapes=[
            pltpu.VMEM((1, nodes), jnp.float32),
            pltpu.VMEM((1, nodes), jnp.float32),
            pltpu.VMEM((slots, BLOCK, BLOCK), jnp.float32),
            pltpu.SMEM((1, slots), jnp.int32),
            pltpu.SMEM((1, slots), jnp.int32),
            pltpu.VMEM((slots * BLOCK, nodes), jnp.bfloat16),
            pltpu.VMEM((chunk, slots * BLOCK), jnp.bfloat16),
            pltpu.VMEM((size, count * owned, PIECE), jnp.bfloat16),
            pltpu.VMEM((4, 8, 128), jnp.int32),
            pltpu.SMEM((4, 8, 128), jnp.int32),
            pltpu.VMEM((bins, BLOCK), jnp.float32),
            pltpu.VMEM((bins, BLOCK), jnp.float32),
            pltpu.VMEM((bins, hidden_size), jnp.bfloat16),
            pltpu.VMEM((hidden_size, bins), jnp.bfloat16),
            pltpu.VMEM((bins, hidden_size), jnp.bfloat16),
            pltpu.SemaphoreType.DMA((chunks, 4)),
            pltpu.SemaphoreType.DMA((chunks, 4)),
            pltpu.SemaphoreType.DMA((4,)),
            pltpu.SemaphoreType.DMA((4,)),
            pltpu.SemaphoreType.DMA((size,)),
            pltpu.SemaphoreType.DMA((size,)),
            pltpu.SemaphoreType.DMA((8,)),
        ]
        + [pltpu.VMEM((5 * owned, chunk, BLOCK), jnp.bfloat16)] * chunks,
        compiler_params=pltpu.CompilerParams(
            collective_id=0, has_side_effects=True, vmem_limit_bytes=48 * 2**20
        ),
        name="exchange",
    )(
        wave_state.T,
        pool_weight.reshape(1, nodes),
        lift_weight.reshape(1, nodes),
        mixing,
        block_matrix[0],
        edge_dst,
        edge_src,
        edge_count,
        lists,
        gain_row,
        proj_in,
        proj_out.T,
    )
    return turned.T


def solution(mesh):
    in_specs = (
        P(("members", "nodes"), None),
        P("nodes"),
        P("nodes"),
        P(),
        P("nodes", None, None, None),
        P("nodes", None),
        P("nodes", None),
        P("nodes"),
        P("nodes", None, None),
        P(),
        P(),
        P(),
    )
    out_specs = P(("members", "nodes"), None)
    return jax.shard_map(
        functools.partial(shards, mesh.shape["nodes"]),
        mesh=mesh,
        in_specs=in_specs,
        out_specs=out_specs,
        check_vma=False,
    )
```
